256 devices in a mesh: replica: 8 (over z), fsdp: 32 (over x, y, core).
Axes of the slice: x: 4, y: 4, z: 8, core: 2. Of those that a mesh axis runs over, the one named last changes fastest.
Arguments:
- grad_parts: bfloat16 [8, 256, 512, 512], P('replica', None, 'fsdp'), may hold values from -6 to 6
- moment: float32 [256, 512, 512], P(('replica', 'fsdp')), may hold values from -4 to 4
- second_moment: float32 [256, 512, 512], P(('replica', 'fsdp')), may hold values from 0.25 to 4
- left_factor: float32 [256, 512, 512], P(('replica', 'fsdp'))
- right_factor: float32 [256, 512, 512], P(('replica', 'fsdp'))
- left_basis: float32 [256, 512, 512], P(('replica', 'fsdp'))
- right_basis: float32 [256, 512, 512], P(('replica', 'fsdp'))
- block_order: int32 [256], replicated, may hold values from 0 to 255, as said below
- refresh_ids: int32 [25], replicated, may hold values from 0 to 249, as said below
Outputs:
- step_dir: bfloat16 [256, 512, 512], P('replica', 'fsdp')
- left_new: float32 [256, 512, 512], P(('replica', 'fsdp'))
- right_new: float32 [256, 512, 512], P(('replica', 'fsdp'))
The draws below stay inside these ranges and needn't reach their ends.
Inputs may be any that keep to these rules, and one draw needn't show every extreme that they name: Slot s holds block block_order[s]; it is a permutation of the 256 blocks in which block_order[s] // 32 == s // 32. refresh_ids[j] lies in [10 j, 10 j + 9]; the ids are distinct and rising; the first is 0 and the last is 249.
All inputs are finite; a program needn't handle non-finite values.
Results may differ from the reference program's by a relative error of at most 0.011.
Values may be sent and summed in bfloat16 or wider, within the bound.
A program may use at most 128 MiB of HBM per device.

```python
import math
import jax
import jax.numpy as jnp
from jax import lax

B = 512
GB = 32
NB = 256
NREF = 25
N_REPLICA = 8


def butterfly_rows(matrix, angles):
    size = matrix.shape[0]
    for section in range(angles.shape[0]):
        half = 2 ** section
        shaped = matrix.reshape(size // (2 * half), 2, half, -1)
        upper = shaped[:, 0]
        lower = shaped[:, 1]
        theta = angles[section].reshape(size // (2 * half), half, 1)
        cosine = jnp.cos(theta)
        sine = jnp.sin(theta)
        matrix = jnp.stack([cosine * upper - sine * lower, sine * upper + cosine * lower], axis=1).reshape(size, -1)
    return matrix


def draw_basis(key):
    sections = B.bit_length() - 1
    angles = jax.random.uniform(key, (NB, sections, B // 2), jnp.float32, -math.pi, math.pi)
    identity = jnp.eye(B, dtype=jnp.float32)
    return jax.vmap(lambda angle_set: butterfly_rows(identity, angle_set))(angles)


def draw_factor(key, spectrum):
    sections = B.bit_length() - 1
    angles = jax.random.uniform(key, (NB, sections, B // 2), jnp.float32, -math.pi, math.pi)
    identity = jnp.eye(B, dtype=jnp.float32)

    def build(angle_set, values):
        rotated = butterfly_rows(identity * values[None, :], angle_set)
        both = butterfly_rows(rotated.T, angle_set)
        return 0.5 * (both + both.T)
    return jax.vmap(build)(angles, spectrum)


def draw_left_factor(key, part):
    key = jax.random.fold_in(key, 3)
    first, second = jax.random.split(key)
    spectrum = jnp.exp(jax.random.uniform(second, (NB, B), jnp.float32, math.log(2.0), math.log(20.0)))
    return draw_factor(first, spectrum)


def draw_right_factor(key, part):
    key = jax.random.fold_in(key, 5)
    first, second = jax.random.split(key)
    spectrum = jnp.exp(jax.random.uniform(second, (NB, B), jnp.float32, math.log(2.0), math.log(20.0)))
    return draw_factor(first, spectrum)


def draw_left_basis(key, part):
    key = jax.random.fold_in(key, 7)
    return draw_basis(key)


def draw_right_basis(key, part):
    key = jax.random.fold_in(key, 9)
    return draw_basis(key)


def draw_block_order(key, part):
    key = jax.random.fold_in(key, 11)
    groups = NB // GB
    keys = jax.random.split(key, groups)
    orders = jax.vmap(lambda sub: jax.random.permutation(sub, GB))(keys)
    offsets = (jnp.arange(groups, dtype=jnp.int32) * GB)[:, None]
    return (orders.astype(jnp.int32) + offsets).reshape(-1).astype(jnp.int32)


def draw_refresh_ids(key, part):
    key = jax.random.fold_in(key, 13)
    jitter = jax.random.randint(key, (NREF,), 0, 10, dtype=jnp.int32)
    jitter = jitter.at[0].set(0).at[NREF - 1].set(9)
    return (jnp.arange(NREF, dtype=jnp.int32) * 10 + jitter).astype(jnp.int32)


def level_of(rng, dims, cuts, smallest, top_value):
    def one(dim, shards_of):
        heights = jax.random.uniform(jax.random.fold_in(jax.random.fold_in(rng, 6), dim), (shards_of,), jnp.float32, smallest / len(cuts), top_value / len(cuts))
        return jnp.repeat(jnp.exp(heights), dims[dim] // shards_of).reshape((-1,) + (1,) * (len(dims) - dim - 1))

    loudness = one(*cuts[0])
    for cut in cuts[1:]:
        loudness = loudness * one(*cut)
    return loudness


def noise(own_key, shape, spread, most, cuts=(), kind=jnp.bfloat16):
    entries = jax.random.normal(own_key, shape, jnp.float32) * spread
    if len(cuts) > 0:
        entries = level_of(own_key, shape, cuts, -0.22, 0.18) * entries
    return jnp.clip(entries, min=-most, max=most).astype(kind)


def setup_inputs(seed: int = 0) -> dict:
    arg_keys = jax.random.split(jax.random.key(seed), 10)
    return {
        "grad_parts": noise(arg_keys[0], (N_REPLICA, NB, B, B), 1.0, 6.0, ((0, 8), (2, 32))),
        "moment": noise(arg_keys[1], (NB, B, B), 0.3, 4.0, ((0, 256),), jnp.float32),
        "second_moment": jnp.clip(jnp.exp(math.log(4.0) - 2.7725887 * jax.random.uniform(arg_keys[2], (NB, B, B), jnp.float32) ** level_of(arg_keys[2], (NB, B, B), ((0, 256),), -0.2, 0.2)), 0.25, 4.0),
        "left_factor": draw_left_factor(jax.random.fold_in(arg_keys[9], 71), 0),
        "right_factor": draw_right_factor(jax.random.fold_in(arg_keys[9], 71), 0),
        "left_basis": draw_left_basis(jax.random.fold_in(arg_keys[9], 71), 0),
        "right_basis": draw_right_basis(jax.random.fold_in(arg_keys[9], 71), 0),
        "block_order": draw_block_order(jax.random.fold_in(arg_keys[9], 71), 0),
        "refresh_ids": draw_refresh_ids(jax.random.fold_in(arg_keys[9], 71), 0),
    }


highest = lax.Precision.HIGHEST

def orthonormal(product):
    gram = jnp.dot(product.T, product, precision=highest)
    lower = jnp.linalg.cholesky(gram)
    return jax.scipy.linalg.solve_triangular(lower, product.T, lower=True).T

def soap_block(items):
    gradient, first, second, left_fac, right_fac, left_old, right_old, refresh_flag = items
    left_new = 0.95 * left_fac + 0.05 * jnp.dot(gradient, gradient.T, precision=highest) / B
    right_new = 0.95 * right_fac + 0.05 * jnp.dot(gradient.T, gradient, precision=highest) / B
    left_q = lax.cond(refresh_flag, lambda: orthonormal(jnp.dot(left_new, left_old, precision=highest)), lambda: left_old)
    right_q = lax.cond(refresh_flag, lambda: orthonormal(jnp.dot(right_new, right_old, precision=highest)), lambda: right_old)
    moment_next = 0.9 * first + 0.1 * gradient
    rot_grad = jnp.dot(jnp.dot(left_q.T, gradient, precision=highest), right_q, precision=highest)
    rot_moment = jnp.dot(jnp.dot(left_q.T, moment_next, precision=highest), right_q, precision=highest)
    second_next = 0.95 * second + 0.05 * rot_grad * rot_grad
    scaled = rot_moment / (jnp.sqrt(second_next) + 1e-08)
    back = jnp.dot(jnp.dot(left_q, scaled, precision=highest), right_q.T, precision=highest)
    return (back.astype(jnp.bfloat16), left_new, right_new)

def reference(grad_parts, moment, second_moment, left_factor, right_factor, left_basis, right_basis, block_order, refresh_ids):
    grad = lax.optimization_barrier(jnp.sum(grad_parts, axis=0, dtype=jnp.float32))
    slot_grad = jnp.take(grad, block_order, axis=0)
    refresh_flags = jnp.any(block_order[:, None] == refresh_ids[None, :], axis=1)
    slot_update, left_new, right_new = lax.map(soap_block, (slot_grad, moment, second_moment, left_factor, right_factor, left_basis, right_basis, refresh_flags))
    step_dir = jnp.zeros_like(slot_update).at[block_order].set(slot_update)
    return (step_dir, left_new, right_new)
```

```python
import functools

import jax
import jax.numpy as jnp
from jax import lax
from jax.experimental import pallas as pl
from jax.experimental.pallas import tpu as pltpu
from jax.sharding import PartitionSpec as P

MESH = pl.DeviceIdType.MESH
f32 = jnp.float32
bf16 = jnp.bfloat16

PIECES = 4
DOWN, UP = 0, 1
LONG, SHORT = 0, 1
HOPS = (4, 3)


def greet(partners):
    barrier = pltpu.get_barrier_semaphore()
    for partner in partners:
        pl.semaphore_signal(barrier, inc=1, device_id=partner, device_id_type=MESH)


def gather_kernel(nz, nf, order_ref, parts_ref, grad_ref, own, first, arms, out, load_sem,
                  arm_send, arm_recv, out_send, out_recv):
    z = lax.axis_index("replica")
    f = lax.axis_index("fsdp")
    group = own.shape[0] // nz
    half = group // 2
    per = half // PIECES
    rows = own.shape[1]

    loads = [
        pltpu.make_async_copy(
            parts_ref.at[0, pl.ds(g * group, group)], own.at[pl.ds(g * group, group)], load_sem.at[g]
        )
        for g in range(nz)
    ]
    for load in loads:
        load.start()

    barrier = pltpu.get_barrier_semaphore()
    for step in (1, nz - 1):
        pl.semaphore_signal(
            barrier, inc=1, device_id=(lax.rem(z + step, nz), f), device_id_type=MESH
        )

    def hello(i, c):
        pl.semaphore_signal(
            barrier, inc=1, device_id=(z, lax.rem(f + i, nf)), device_id_type=MESH
        )
        return c

    lax.fori_loop(1, nf, hello, 0)
    for load in loads:
        load.wait()
    pl.semaphore_wait(barrier, nf + 1)

    def mine(dest, i):
        slot = lax.rem(f + i, nf)
        return own[order_ref[dest * group + slot]]

    def half_of(way, arm):
        return way ^ arm

    def copy(way, arm, hop, p):
        src = first.at[way, arm] if hop == 0 else arms.at[way, arm, hop - 1]
        step = nz - 1 if way == DOWN else 1
        piece = pl.ds(p * per, per)
        return pltpu.make_async_remote_copy(
            src_ref=src.at[piece],
            dst_ref=arms.at[way, arm, hop].at[piece],
            send_sem=arm_send.at[way, arm, hop, p],
            recv_sem=arm_recv.at[way, arm, hop, p],
            device_id=(lax.rem(z + step, nz), f),
            device_id_type=MESH,
        )

    def target(way, arm, hop):
        left = HOPS[arm] - hop
        return lax.rem(z + (nz - left if way == DOWN else left), nz)

    for hop in range(4):

        def piece_step(p, c):
            for arm in (LONG, SHORT):
                if hop >= HOPS[arm]:
                    continue
                for way in (DOWN, UP):
                    if hop > 0:
                        copy(way, arm, hop - 1, p).wait_recv()
                    dest = target(way, arm, hop)
                    start = half_of(way, arm) * half

                    def slot_step(k, c):
                        i = p * per + k
                        value = mine(dest, start + i)
                        if hop == 0:
                            first[way, arm, i] = value
                        else:
                            total = arms[way, arm, hop - 1, i].astype(f32) + value.astype(f32)
                            arms[way, arm, hop - 1, i] = total.astype(bf16)
                        return c

                    lax.fori_loop(0, per, slot_step, 0)
                    copy(way, arm, hop, p).start()
            return c

        lax.fori_loop(0, PIECES, piece_step, 0)

    def send_out(i):
        peer = lax.rem(f + i, nf)
        return pltpu.make_async_remote_copy(
            src_ref=out.at[i],
            dst_ref=grad_ref.at[pl.ds(pl.multiple_of(f * rows, rows), rows)],
            send_sem=out_send.at[i],
            recv_sem=out_recv.at[i],
            device_id=(z, peer),
            device_id_type=MESH,
        )

    def finish(p, c):
        for part in range(2):
            long_way = DOWN if part == 0 else UP
            short_way = UP if part == 0 else DOWN
            copy(long_way, LONG, 3, p).wait_recv()
            copy(short_way, SHORT, 2, p).wait_recv()

            def slot_step(k, c):
                i = p * per + k
                total = (
                    arms[long_way, LONG, 3, i].astype(f32)
                    + arms[short_way, SHORT, 2, i].astype(f32)
                    + mine(z, part * half + i).astype(f32)
                ).astype(bf16)
                j = part * half + i
                out[j] = total

                @pl.when(j == 0)
                def _():
                    grad_ref[pl.ds(pl.multiple_of(f * rows, rows), rows)] = total

                @pl.when(j > 0)
                def _():
                    send_out(j).start()

                return c

            lax.fori_loop(0, per, slot_step, 0)
        return c

    lax.fori_loop(0, PIECES, finish, 0)

    def drain(i, c):
        send_out(i).wait_send()
        send_out(i).wait_recv()
        return c

    lax.fori_loop(1, nf, drain, 0)

    for hop in range(4):
        for arm in (LONG, SHORT):
            if hop < HOPS[arm]:
                for way in (DOWN, UP):

                    def sent(p, c):
                        copy(way, arm, hop, p).wait_send()
                        return c

                    lax.fori_loop(0, PIECES, sent, 0)


def gather(nz, nf, order, parts):
    _, blocks, rows, width = parts.shape
    half = blocks // nz // 2
    return pl.pallas_call(
        functools.partial(gather_kernel, nz, nf),
        out_shape=jax.ShapeDtypeStruct((nf * rows, width), bf16),
        in_specs=[
            pl.BlockSpec(memory_space=pltpu.SMEM),
            pl.BlockSpec(memory_space=pl.ANY),
        ],
        out_specs=pl.BlockSpec(memory_space=pltpu.VMEM),
        scratch_shapes=[
            pltpu.VMEM((blocks, rows, width), bf16),
            pltpu.VMEM((2, 2, half, rows, width), bf16),
            pltpu.VMEM((2, 2, 4, half, rows, width), bf16),
            pltpu.VMEM((2 * half, rows, width), bf16),
            pltpu.SemaphoreType.DMA((nz,)),
            pltpu.SemaphoreType.DMA((2, 2, 4, PIECES)),
            pltpu.SemaphoreType.DMA((2, 2, 4, PIECES)),
            pltpu.SemaphoreType.DMA((nf,)),
            pltpu.SemaphoreType.DMA((nf,)),
        ],
        compiler_params=pltpu.CompilerParams(
            collective_id=0, has_side_effects=True, vmem_limit_bytes=40 * 2**20
        ),
        name="gather_grad",
    )(order, parts)


NB = 64


def split(x):
    high = x.astype(bf16)
    return high, (x - high.astype(f32)).astype(bf16)


def dg(a, b, ca, cb):
    return lax.dot_general(a, b, (((ca,), (cb,)), ((), ())), preferred_element_type=f32)


def dot3(a, b, ca=1, cb=0):
    return dg(a[0], b[0], ca, cb) + (dg(a[0], b[1], ca, cb) + dg(a[1], b[0], ca, cb))


def lanes(x, at):
    return [
        jnp.take_along_axis(x, jnp.full(x.shape, at + j, jnp.int32), axis=1) for j in range(8)
    ]


def spread(x, j):
    return jnp.broadcast_to(x[j : j + 1, :], x.shape)


def pivot_rows(e_ref, m, at):
    sub = lax.broadcasted_iota(jnp.int32, (8, 128), 0)
    piv = e_ref[m, at : at + 8, :]
    b = lanes(piv, at)
    diag = None
    inverse, above, pivots = [], [], []
    for j in range(8):
        d = spread(b[j], j)
        diag = d if diag is None else jnp.where(sub == j, d, diag)
        r = 1.0 / d
        inverse.append(r)
        factor = jnp.where(sub > j, b[j] * r, 0.0)
        row = {}
        for t in range(j + 1, 8):
            row[t] = spread(b[t], j)
            b[t] = b[t] - factor * row[t]
        above.append(row)
        pivots.append(spread(piv, j))
        piv = piv - factor * pivots[j]
    return inverse, above, pivots, piv * lax.rsqrt(diag)


def chol_inverse(e_ref):
    for at in range(0, NB, 8):
        found = [pivot_rows(e_ref, m, at) for m in range(2)]
        for m in range(2):
            inverse, above, pivots, piv = found[m]
            for i in range(at + 8, NB, 8):
                x = e_ref[m, i : i + 8, :]
                b = lanes(x, at)
                for j in range(8):
                    factor = b[j] * inverse[j]
                    for t in range(j + 1, 8):
                        b[t] = b[t] - factor * above[j][t]
                    x = x - factor * pivots[j]
                e_ref[m, i : i + 8, :] = x
            e_ref[m, at : at + 8, :] = piv


def orthonormal(a_ref, t_ref, e_ref):
    size = a_ref.shape[1]
    eye = (
        lax.broadcasted_iota(jnp.int32, (NB, NB), 0) == lax.broadcasted_iota(jnp.int32, (NB, NB), 1)
    ).astype(f32)
    for o in range(0, size, NB):
        n = o + NB
        for m in range(2):
            e_ref[m, :, :NB] = a_ref[m, o:n, o:n]
            e_ref[m, :, NB:] = eye
        chol_inverse(e_ref)
        for m in range(2):
            w = split(e_ref[m, :, NB:])
            t = dot3(w, split(t_ref[m, o:n, :]))
            t_ref[m, o:n, :] = t
            if n < size:
                u = split(dot3(w, split(a_ref[m, o:n, n:])))
                a_ref[m, n:, n:] = a_ref[m, n:, n:] - dot3(u, u, 0, 0)
                t_ref[m, n:, :] = t_ref[m, n:, :] - dot3(u, split(t), 0, 0)


def step_kernel(order_ref, ids_ref, grad_ref, mom_hbm, sec_hbm, lf_hbm, rf_hbm, lb_hbm, rb_hbm,
                update_ref, ln_hbm, rn_hbm, mom, sec, fac, bas, new, a_ref, t_ref, e_ref,
                in_sem, out_sem):
    nf = 32
    slot = lax.axis_index("replica") * nf + lax.axis_index("fsdp")
    width = grad_ref.shape[1]
    loads = [
        pltpu.make_async_copy(src.at[0], dst, in_sem.at[n])
        for n, (src, dst) in enumerate(
            (
                (lf_hbm, fac.at[0]),
                (rf_hbm, fac.at[1]),
                (lb_hbm, bas.at[0]),
                (rb_hbm, bas.at[1]),
                (mom_hbm, mom),
                (sec_hbm, sec),
            )
        )
    ]
    for load in loads:
        load.start()
    block = order_ref[slot]
    flag = lax.fori_loop(
        0, ids_ref.shape[0], lambda i, c: c | (ids_ref[i] == block).astype(jnp.int32), jnp.int32(0)
    )
    grad = grad_ref[...]
    stores = []
    for m, hbm in enumerate((ln_hbm, rn_hbm)):
        loads[m].wait()
        new[m] = 0.95 * fac[m] + (0.05 / width) * dg(grad, grad, 1 - m, 1 - m)
        stores.append(pltpu.make_async_copy(new.at[m], hbm.at[0], out_sem.at[m]))
        stores[m].start()
    loads[2].wait()
    loads[3].wait()

    @pl.when(flag == 1)
    def _():
        for m in range(2):
            t = dot3(split(bas[m]), split(new[m]), 0, 1)
            t_ref[m] = t
            s = split(t)
            a_ref[m] = dot3(s, s, 1, 1)
        orthonormal(a_ref, t_ref, e_ref)
        for m in range(2):
            bas[m] = t_ref[m].T

    loads[4].wait()
    loads[5].wait()
    lq = split(bas[0])
    rq = split(bas[1])
    moment = split(0.9 * mom[...] + 0.1 * grad.astype(f32))
    half_grad = split(dg(lq[0], grad, 0, 0) + dg(lq[1], grad, 0, 0))
    half_mom = split(dot3(lq, moment, 0, 0))
    rot_grad = dot3(half_grad, rq)
    rot_mom = dot3(half_mom, rq)
    second = 0.95 * sec[...] + 0.05 * rot_grad * rot_grad
    scaled = split(rot_mom / (jnp.sqrt(second) + 1e-08))
    back = split(dot3(lq, scaled))
    update_ref[...] = dot3(back, rq, 1, 1).astype(bf16)
    for store in stores:
        store.wait()


def step(order, ids, grad, moment, second, lf, rf, lb, rb):
    width = grad.shape[1]
    square = pltpu.VMEM((width, width), f32)
    pair = pltpu.VMEM((2, width, width), f32)
    smem = pl.BlockSpec(memory_space=pltpu.SMEM)
    vmem = pl.BlockSpec(memory_space=pltpu.VMEM)
    hbm = pl.BlockSpec(memory_space=pl.ANY)
    whole = jax.ShapeDtypeStruct((1, width, width), f32)
    return pl.pallas_call(
        step_kernel,
        out_shape=(jax.ShapeDtypeStruct((width, width), bf16), whole, whole),
        in_specs=[smem, smem, vmem] + [hbm] * 6,
        out_specs=(vmem, hbm, hbm),
        scratch_shapes=[
            square,
            square,
            pair,
            pair,
            pair,
            pair,
            pair,
            pltpu.VMEM((2, NB, 2 * NB), f32),
            pltpu.SemaphoreType.DMA((6,)),
            pltpu.SemaphoreType.DMA((2,)),
        ],
        compiler_params=pltpu.CompilerParams(vmem_limit_bytes=50 * 2**20),
        name="block_step",
    )(order, ids, grad, moment, second, lf, rf, lb, rb)


def scatter_kernel(nf, where_ref, update_ref, out_ref, held, send_sem, recv_sem):
    z = lax.axis_index("replica")
    f = lax.axis_index("fsdp")
    rows = out_ref.shape[1]
    barrier = pltpu.get_barrier_semaphore()

    def hello(i, c):
        pl.semaphore_signal(
            barrier, inc=1, device_id=(z, lax.rem(f + i, nf)), device_id_type=MESH
        )
        return c

    lax.fori_loop(1, nf, hello, 0)
    pl.semaphore_wait(barrier, nf - 1)

    def copy(i):
        peer = lax.rem(f + i, nf)
        return pltpu.make_async_remote_copy(
            src_ref=update_ref.at[pl.ds(pl.multiple_of(peer * rows, rows), rows)],
            dst_ref=held.at[f],
            send_sem=send_sem.at[i],
            recv_sem=recv_sem.at[i],
            device_id=(z, peer),
            device_id_type=MESH,
        )

    def begin(i, c):
        copy(i).start()
        return c

    def drain(i, c):
        copy(i).wait()
        return c

    def place(i, c):
        out_ref[i] = held[where_ref[i]]
        return c

    lax.fori_loop(1, nf, begin, 0)
    held[f] = update_ref[pl.ds(pl.multiple_of(f * rows, rows), rows)]
    lax.fori_loop(1, nf, drain, 0)
    lax.fori_loop(0, nf, place, 0)


def scatter(nf, where, update):
    width = update.shape[1]
    rows = update.shape[0] // nf
    return pl.pallas_call(
        functools.partial(scatter_kernel, nf),
        out_shape=jax.ShapeDtypeStruct((nf, rows, width), bf16),
        in_specs=[
            pl.BlockSpec(memory_space=pltpu.SMEM),
            pl.BlockSpec(memory_space=pltpu.VMEM),
        ],
        out_specs=pl.BlockSpec(memory_space=pltpu.VMEM),
        scratch_shapes=[
            pltpu.VMEM((nf, rows, width), bf16),
            pltpu.SemaphoreType.DMA((nf,)),
            pltpu.SemaphoreType.DMA((nf,)),
        ],
        compiler_params=pltpu.CompilerParams(collective_id=1, has_side_effects=True),
        name="scatter_update",
    )(where, update)


def solution(mesh):
    nz, nf = mesh.shape["replica"], mesh.shape["fsdp"]

    def on_device(parts, moment, second, lf, rf, lb, rb, order, ids):
        group = parts.shape[1] // nz
        start = lax.axis_index("replica") * group
        local = lax.dynamic_slice_in_dim(order, start, group) - start
        blocks = jnp.arange(group, dtype=jnp.int32)
        where = jnp.sum(jnp.where(local[None, :] == blocks[:, None], blocks[None, :], 0), axis=1)
        grad = gather(nz, nf, order, parts)
        update, left_new, right_new = step(order, ids, grad, moment, second, lf, rf, lb, rb)
        return scatter(nf, where, update), left_new, right_new

    placed = (P("replica", None, "fsdp", None),) + (P(("replica", "fsdp"), None, None),) * 6 + (P(), P())
    return jax.shard_map(
        on_device,
        mesh=mesh,
        in_specs=placed,
        out_specs=(
            P("replica", "fsdp", None),
            P(("replica", "fsdp"), None, None),
            P(("replica", "fsdp"), None, None),
        ),
        check_vma=False,
    )
```

```python
import functools

import jax
import jax.numpy as jnp
from jax import lax
from jax.experimental import pallas as pl
from jax.experimental.pallas import tpu as pltpu
from jax.sharding import PartitionSpec as P

MESH = pl.DeviceIdType.MESH
f32 = jnp.float32
bf16 = jnp.bfloat16

DOWN, UP = 0, 1
LONG, SHORT = 0, 1
HOPS = (4, 3)
EARLY = 4
DECADE = 10
PER = 2
NB = 64


def split(x):
    high = x.astype(bf16)
    return high, (x - high.astype(f32)).astype(bf16)


def dg(a, b, ca=1, cb=0):
    return lax.dot_general(a, b, (((ca,), (cb,)), ((), ())), preferred_element_type=f32)


def dot3(a, b, ca=1, cb=0):
    return dg(a[0], b[0], ca, cb) + (dg(a[0], b[1], ca, cb) + dg(a[1], b[0], ca, cb))


def lanes(x, at):
    return [
        jnp.take_along_axis(x, jnp.full(x.shape, at + j, jnp.int32), axis=1) for j in range(8)
    ]


def spread(x, j):
    return jnp.broadcast_to(x[j : j + 1, :], x.shape)


def pivot_rows(e_ref, m, at):
    sub = lax.broadcasted_iota(jnp.int32, (8, 128), 0)
    piv = e_ref[m, at : at + 8, :]
    b = lanes(piv, at)
    diag = None
    inverse, above, pivots = [], [], []
    for j in range(8):
        d = spread(b[j], j)
        diag = d if diag is None else jnp.where(sub == j, d, diag)
        r = 1.0 / d
        inverse.append(r)
        factor = jnp.where(sub > j, b[j] * r, 0.0)
        row = {}
        for t in range(j + 1, 8):
            row[t] = spread(b[t], j)
            b[t] = b[t] - factor * row[t]
        above.append(row)
        pivots.append(spread(piv, j))
        piv = piv - factor * pivots[j]
    return inverse, above, pivots, piv * lax.rsqrt(diag)


def chol_inverse(e_ref):
    for at in range(0, NB, 8):
        found = [pivot_rows(e_ref, m, at) for m in range(2)]
        for m in range(2):
            inverse, above, pivots, piv = found[m]
            for i in range(at + 8, NB, 8):
                x = e_ref[m, i : i + 8, :]
                b = lanes(x, at)
                for j in range(8):
                    factor = b[j] * inverse[j]
                    for t in range(j + 1, 8):
                        b[t] = b[t] - factor * above[j][t]
                    x = x - factor * pivots[j]
                e_ref[m, i : i + 8, :] = x
            e_ref[m, at : at + 8, :] = piv


def orthonormal(a_ref, t_ref, e_ref, between):
    size = a_ref.shape[1]
    eye = (
        lax.broadcasted_iota(jnp.int32, (NB, NB), 0) == lax.broadcasted_iota(jnp.int32, (NB, NB), 1)
    ).astype(f32)
    for o in range(0, size, NB):
        n = o + NB
        for m in range(2):
            e_ref[m, :, :NB] = a_ref[m, o:n, o:n]
            e_ref[m, :, NB:] = eye
        chol_inverse(e_ref)
        between()
        for m in range(2):
            w = split(e_ref[m, :, NB:])
            t = dot3(w, split(t_ref[m, o:n, :]))
            t_ref[m, o:n, :] = t
            if n < size:
                u = split(dot3(w, split(a_ref[m, o:n, n:])))
                a_ref[m, n:, n:] = a_ref[m, n:, n:] - dot3(u, u, 0, 0)
                t_ref[m, n:, :] = t_ref[m, n:, :] - dot3(u, split(t), 0, 0)
        between()


def main_kernel(
    nz, nf, order_ref, ids_ref, parts_hbm, mom_hbm, sec_hbm, lf_hbm, rf_hbm, lb_hbm, rb_hbm,
    held, grad,
    own, first_a, arms_a, first_b, arms_b, acc, out_a, grad_a, out_b, update,
    fac, bas, new, a_ref, t_ref, mom, sec, rotated, lq, rq, e_ref, back_hi,
    load_sem, send_a, recv_a, send_b, recv_b, give_a, take_a, give_b, take_b, give_c, take_c,
):
    z = lax.axis_index("replica")
    f = lax.axis_index("fsdp")
    group = own.shape[0] // nz
    rows, width = own.shape[1:]
    nref = ids_ref.shape[0]

    loads = [
        pltpu.make_async_copy(
            parts_hbm.at[0, pl.ds(g * group, group)], own.at[pl.ds(g * group, group)], load_sem.at[g]
        )
        for g in range(nz)
    ]
    places = (
        (lf_hbm, fac.at[0]),
        (rf_hbm, fac.at[1]),
        (lb_hbm, bas.at[0]),
        (rb_hbm, bas.at[1]),
        (mom_hbm, mom),
        (sec_hbm, sec),
    )
    later = [
        pltpu.make_async_copy(src.at[0], dst, load_sem.at[nz + n])
        for n, (src, dst) in enumerate(places)
    ]
    for load in loads + later:
        load.start()

    barrier = pltpu.get_barrier_semaphore()
    for step in (1, nz - 1):
        pl.semaphore_signal(
            barrier, inc=1, device_id=(lax.rem(z + step, nz), f), device_id_type=MESH
        )

    def hello(i, c):
        pl.semaphore_signal(
            barrier, inc=1, device_id=(z, lax.rem(f + i, nf)), device_id_type=MESH
        )
        return c

    lax.fori_loop(1, nf, hello, 0)

    def early(g):
        start = (g * group) // DECADE
        found = []
        for c in range(EARLY):
            at = start + c
            block = jnp.where(at < nref, ids_ref[jnp.minimum(at, nref - 1)], nz * group)
            found.append(jnp.clip(block - g * group, 0, group - 1))
        return found

    def late(found, q):
        block = q
        for a in found:
            block = block + (block >= a).astype(jnp.int32)
        return block

    own_early = early(z)

    def position(block):
        block = jnp.clip(block, 0, group - 1)
        below = sum((a < block).astype(jnp.int32) for a in own_early)
        same = sum((a == block).astype(jnp.int32) for a in own_early)
        return jnp.where(same > 0, below, EARLY + block - below)

    for load in loads:
        load.wait()
    pl.semaphore_wait(barrier, nf + 1)

    def target(way, arm, hop):
        left = HOPS[arm] - hop
        return lax.rem(z + (nz - left if way == DOWN else left), nz)

    def ring_copy(stage, way, arm, hop, p):
        first, arms, send, recv = stage
        src = first.at[way, arm] if hop == 0 else arms.at[way, arm, hop - 1]
        step = nz - 1 if way == DOWN else 1
        piece = pl.ds(p * PER, PER)
        return pltpu.make_async_remote_copy(
            src_ref=src.at[piece],
            dst_ref=arms.at[way, arm, hop].at[piece],
            send_sem=send.at[way, arm, hop, p],
            recv_sem=recv.at[way, arm, hop, p],
            device_id=(lax.rem(z + step, nz), f),
            device_id_type=MESH,
        )

    def block_at(stage, dest, part, i):
        found = early(dest)
        if stage is ring_a:
            return dest * group + found[part * (EARLY // 2) + i]
        return dest * group + late(found, part * ((group - EARLY) // 2) + i)

    def ring_step(stage, hop, p):
        first, arms = stage[:2]
        for arm in (LONG, SHORT):
            if hop >= HOPS[arm]:
                continue
            for way in (DOWN, UP):
                if hop > 0:
                    ring_copy(stage, way, arm, hop - 1, p).wait_recv()
                dest = target(way, arm, hop)
                for k in range(PER):
                    i = p * PER + k
                    value = own[block_at(stage, dest, way ^ arm, i)]
                    if hop == 0:
                        first[way, arm, i] = value
                    else:
                        total = arms[way, arm, hop - 1, i].astype(f32) + value.astype(f32)
                        arms[way, arm, hop - 1, i] = total.astype(bf16)
                ring_copy(stage, way, arm, hop, p).start()

    def ring_end(stage, p):
        arms = stage[1]
        base = 0 if stage is ring_a else EARLY
        count = EARLY // 2 if stage is ring_a else (group - EARLY) // 2
        for part in range(2):
            long_way, short_way = (DOWN, UP) if part == 0 else (UP, DOWN)
            ring_copy(stage, long_way, LONG, 3, p).wait_recv()
            ring_copy(stage, short_way, SHORT, 2, p).wait_recv()
            for k in range(PER):
                i = p * PER + k
                total = (
                    arms[long_way, LONG, 3, i].astype(f32)
                    + arms[short_way, SHORT, 2, i].astype(f32)
                    + own[block_at(stage, z, part, i)].astype(f32)
                )
                acc[base + part * count + i] = total.astype(bf16)

    def ring_sent(stage, pieces):
        for hop in range(4):
            for arm in (LONG, SHORT):
                if hop < HOPS[arm]:
                    for way in (DOWN, UP):

                        def sent(p, c):
                            ring_copy(stage, way, arm, hop, p).wait_send()
                            return c

                        lax.fori_loop(0, pieces, sent, 0)

    ring_a = (first_a, arms_a, send_a, recv_a)
    ring_b = (first_b, arms_b, send_b, recv_b)
    pieces = (group - EARLY) // 2 // PER
    todo = [functools.partial(ring_step, ring_b, hop, p) for hop in range(4) for p in range(pieces)]
    todo += [functools.partial(ring_end, ring_b, p) for p in range(pieces)]
    todo.reverse()

    def pump(n=1):
        for _ in range(n):
            if todo:
                todo.pop()()

    mine = pl.ds(pl.multiple_of(f * rows, rows), rows)

    def give(out, into, send, recv, i):
        return pltpu.make_async_remote_copy(
            src_ref=out.at[i],
            dst_ref=into.at[mine],
            send_sem=send.at[i],
            recv_sem=recv.at[i],
            device_id=(z, lax.rem(f + i, nf)),
            device_id_type=MESH,
        )

    def to_owners(out, into, send, recv, limit):
        def one(i, c):
            slot = lax.rem(f + i, nf)
            at = jnp.minimum(position(order_ref[z * group + slot] - z * group), limit)
            out[i] = acc[at]
            give(out, into, send, recv, i).start()
            return c

        lax.fori_loop(1, nf, one, 0)
        at = jnp.minimum(position(order_ref[z * group + f] - z * group), limit)
        into[mine] = acc[at]

    def from_all(out, into, send, recv):
        def one(i, c):
            give(out, into, send, recv, i).wait_recv()
            return c

        lax.fori_loop(1, nf, one, 0)

    ring_step(ring_a, 0, 0)
    pump(2)
    ring_step(ring_a, 1, 0)
    pump(1)
    ring_step(ring_a, 2, 0)
    pump(2)
    ring_step(ring_a, 3, 0)
    pump(2)
    ring_end(ring_a, 0)
    to_owners(out_a, grad_a, give_a, take_a, EARLY - 1)
    pump(4)
    for load in later:
        load.wait()
    from_all(out_a, grad_a, give_a, take_a)

    g_a = grad_a[...]
    for m in range(2):
        new[m] = 0.95 * fac[m] + (0.05 / width) * dg(g_a, g_a, 1 - m, 1 - m)
    pump()
    for m in range(2):
        t_ref[m] = dot3(split(bas[m]), split(new[m]), 0, 1)
    pump()
    for m in range(2):
        s = split(t_ref[m])
        a_ref[m] = dot3(s, s, 1, 1)
    pump()
    orthonormal(a_ref, t_ref, e_ref, pump)
    pump(len(todo))
    to_owners(out_b, grad, give_b, take_b, group - 1)

    block = order_ref[z * group + f]
    flag = lax.fori_loop(
        0, nref, lambda i, c: c | (ids_ref[i] == block).astype(jnp.int32), jnp.int32(0)
    )
    refreshed = jnp.full((width, width), flag, jnp.int32) == 1
    for m, q in enumerate((lq, rq)):
        q[0], q[1] = split(jnp.where(refreshed, t_ref[m].T, bas[m]))
    left = (lq[0], lq[1])
    right = (rq[0], rq[1])
    rotated[...] = 0.9 * dot3(split(dot3(left, split(mom[...]), 0, 0)), right)
    from_all(out_b, grad, give_b, take_b)

    g = grad[...]
    turned = (dg(left[0], g, 0, 0) + dg(left[1], g, 0, 0)).astype(bf16)
    rot_grad = dg(turned, right[0]) + dg(turned, right[1])
    second = 0.95 * sec[...] + 0.05 * rot_grad * rot_grad
    scaled = ((rotated[...] + 0.1 * rot_grad) / (jnp.sqrt(second) + 1e-08)).astype(bf16)
    back_hi[...] = (dg(left[0], scaled) + dg(left[1], scaled)).astype(bf16)

    quarter = nf // 4

    def give_back(peer):
        there = pl.ds(pl.multiple_of(peer * rows, rows), rows)
        i = lax.rem(peer - f + nf, nf)
        return pltpu.make_async_remote_copy(
            src_ref=update.at[there],
            dst_ref=held.at[f],
            send_sem=give_c.at[i],
            recv_sem=take_c.at[i],
            device_id=(z, peer),
            device_id_type=MESH,
        )

    def some_rows(r, c):
        at = lax.rem(f // quarter + r, 4)
        span = pl.ds(pl.multiple_of(at * quarter * rows, quarter * rows), quarter * rows)
        chunk = back_hi[span]
        update[span] = (dg(chunk, rq[0], 1, 1) + dg(chunk, rq[1], 1, 1)).astype(bf16)

        def one(i, c):
            peer = at * quarter + lax.rem(f + i, quarter)

            @pl.when(peer != f)
            def _():
                give_back(peer).start()

            return c

        lax.fori_loop(0, quarter, one, 0)
        return c

    lax.fori_loop(0, 4, some_rows, 0)
    held[f] = update[mine]

    ring_sent(ring_a, 1)
    ring_sent(ring_b, pieces)

    def drain(i, c):
        give(out_a, grad_a, give_a, take_a, i).wait_send()
        give(out_b, grad, give_b, take_b, i).wait_send()
        peer = lax.rem(f + i, nf)
        give_back(peer).wait_send()
        give_back(peer).wait_recv()
        return c

    lax.fori_loop(1, nf, drain, 0)


def main(nz, nf, order, ids, parts, *rest):
    _, blocks, rows, width = parts.shape
    group = blocks // nz
    smem = pl.BlockSpec(memory_space=pltpu.SMEM)
    vmem = pl.BlockSpec(memory_space=pltpu.VMEM)
    hbm = pl.BlockSpec(memory_space=pl.ANY)
    square = pltpu.VMEM((width, width), f32)
    pair = pltpu.VMEM((2, width, width), f32)
    pair16 = pltpu.VMEM((2, width, width), bf16)
    square16 = pltpu.VMEM((width, width), bf16)
    slots = pltpu.VMEM((nf, rows, width), bf16)
    half_a, half_b = EARLY // 2, (group - EARLY) // 2
    ring = pltpu.SemaphoreType.DMA
    return pl.pallas_call(
        functools.partial(main_kernel, nz, nf),
        out_shape=(
            jax.ShapeDtypeStruct((nf, rows, width), bf16),
            jax.ShapeDtypeStruct((width, width), bf16),
        ),
        in_specs=[smem, smem] + [hbm] * 7,
        out_specs=(vmem, vmem),
        scratch_shapes=[
            pltpu.VMEM((blocks, rows, width), bf16),
            pltpu.VMEM((2, 2, half_a, rows, width), bf16),
            pltpu.VMEM((2, 2, 4, half_a, rows, width), bf16),
            pltpu.VMEM((2, 2, half_b, rows, width), bf16),
            pltpu.VMEM((2, 2, 4, half_b, rows, width), bf16),
            slots,
            slots,
            square16,
            slots,
            square16,
            pair,
            pair,
            pair,
            pair,
            pair,
            square,
            square,
            square,
            pair16,
            pair16,
            pltpu.VMEM((2, NB, 2 * NB), f32),
            square16,
            ring((nz + 6,)),
            ring((2, 2, 4, half_a // PER)),
            ring((2, 2, 4, half_a // PER)),
            ring((2, 2, 4, half_b // PER)),
            ring((2, 2, 4, half_b // PER)),
            ring((nf,)),
            ring((nf,)),
            ring((nf,)),
            ring((nf,)),
            ring((nf,)),
            ring((nf,)),
        ],
        compiler_params=pltpu.CompilerParams(
            collective_id=0, has_side_effects=True, vmem_limit_bytes=59 * 2**20
        ),
        name="soap_step",
    )(order, ids, parts, *rest)


def tail_kernel(nz, nf, order_ref, held, grad_ref, lf_ref, rf_ref, out_hbm, ln_hbm, rn_hbm, new, sem):
    z = lax.axis_index("replica")
    width = grad_ref.shape[1]
    group = held.shape[0]

    def place(i):
        block = jnp.clip(order_ref[z * group + i] - z * group, 0, group - 1)
        return pltpu.make_async_copy(held.at[i], out_hbm.at[block], sem.at[2 + i])

    def begin(i, c):
        place(i).start()
        return c

    def end(i, c):
        place(i).wait()
        return c

    lax.fori_loop(0, nf, begin, 0)
    grad = grad_ref[...]
    stores = []
    for m, (fac, hbm) in enumerate(((lf_ref, ln_hbm), (rf_ref, rn_hbm))):
        new[m] = 0.95 * fac[0] + (0.05 / width) * dg(grad, grad, 1 - m, 1 - m)
        stores.append(pltpu.make_async_copy(new.at[m], hbm.at[0], sem.at[m]))
        stores[m].start()
    for store in stores:
        store.wait()
    lax.fori_loop(0, nf, end, 0)


def tail(nz, nf, order, held, grad, lf, rf):
    width = grad.shape[1]
    smem = pl.BlockSpec(memory_space=pltpu.SMEM)
    vmem = pl.BlockSpec(memory_space=pltpu.VMEM)
    hbm = pl.BlockSpec(memory_space=pl.ANY)
    whole = jax.ShapeDtypeStruct((1, width, width), f32)
    return pl.pallas_call(
        functools.partial(tail_kernel, nz, nf),
        out_shape=(jax.ShapeDtypeStruct(held.shape, bf16), whole, whole),
        in_specs=[smem, vmem, vmem, vmem, vmem],
        out_specs=(hbm, hbm, hbm),
        scratch_shapes=[
            pltpu.VMEM((2, width, width), f32),
            pltpu.SemaphoreType.DMA((2 + nf,)),
        ],
        compiler_params=pltpu.CompilerParams(vmem_limit_bytes=16 * 2**20),
        name="write_out",
    )(order, held, grad, lf, rf)


def solution(mesh):
    nz, nf = mesh.shape["replica"], mesh.shape["fsdp"]

    def on_device(parts, moment, second, lf, rf, lb, rb, order, ids):
        held, grad = main(nz, nf, order, ids, parts, moment, second, lf, rf, lb, rb)
        return tail(nz, nf, order, held, grad, lf, rf)

    placed = (P("replica", None, "fsdp", None),) + (P(("replica", "fsdp"), None, None),) * 6 + (P(), P())
    return jax.shard_map(
        on_device,
        mesh=mesh,
        in_specs=placed,
        out_specs=(
            P("replica", "fsdp", None),
            P(("replica", "fsdp"), None, None),
            P(("replica", "fsdp"), None, None),
        ),
        check_vma=False,
    )
```

```python
import functools

import jax
import jax.numpy as jnp
from jax import lax
from jax.experimental import pallas as pl
from jax.experimental.pallas import tpu as pltpu
from jax.sharding import PartitionSpec as P

MESH = pl.DeviceIdType.MESH
f32 = jnp.float32
bf16 = jnp.bfloat16

DOWN, UP = 0, 1
LONG, SHORT = 0, 1
HOPS = (4, 3)
EARLY = 4
DECADE = 10
PER = 2
NB = 64


def split(x):
    high = x.astype(bf16)
    return high, (x - high.astype(f32)).astype(bf16)


def dg(a, b, ca=1, cb=0):
    return lax.dot_general(a, b, (((ca,), (cb,)), ((), ())), preferred_element_type=f32)


def dot3(a, b, ca=1, cb=0):
    return dg(a[0], b[0], ca, cb) + (dg(a[0], b[1], ca, cb) + dg(a[1], b[0], ca, cb))


def lanes(x, at):
    return [
        jnp.take_along_axis(x, jnp.full(x.shape, at + j, jnp.int32), axis=1) for j in range(8)
    ]


def spread(x, j):
    return jnp.broadcast_to(x[j : j + 1, :], x.shape)


def pivot_rows(e_ref, m, at):
    sub = lax.broadcasted_iota(jnp.int32, (8, 128), 0)
    piv = e_ref[m, at : at + 8, :]
    b = lanes(piv, at)
    diag = None
    inverse, above, pivots = [], [], []
    for j in range(8):
        d = spread(b[j], j)
        diag = d if diag is None else jnp.where(sub == j, d, diag)
        r = 1.0 / d
        inverse.append(r)
        factor = jnp.where(sub > j, b[j] * r, 0.0)
        row = {}
        for t in range(j + 1, 8):
            row[t] = spread(b[t], j)
            b[t] = b[t] - factor * row[t]
        above.append(row)
        pivots.append(spread(piv, j))
        piv = piv - factor * pivots[j]
    return inverse, above, pivots, piv * lax.rsqrt(diag)


def chol_inverse(e_ref):
    for at in range(0, NB, 8):
        found = [pivot_rows(e_ref, m, at) for m in range(2)]
        for m in range(2):
            inverse, above, pivots, piv = found[m]
            for i in range(at + 8, NB, 8):
                x = e_ref[m, i : i + 8, :]
                b = lanes(x, at)
                for j in range(8):
                    factor = b[j] * inverse[j]
                    for t in range(j + 1, 8):
                        b[t] = b[t] - factor * above[j][t]
                    x = x - factor * pivots[j]
                e_ref[m, i : i + 8, :] = x
            e_ref[m, at : at + 8, :] = piv


def orthonormal(a_ref, t_ref, e_ref, w_ref, u_ref, between):
    size = a_ref.shape[1]
    eye = (
        lax.broadcasted_iota(jnp.int32, (NB, NB), 0) == lax.broadcasted_iota(jnp.int32, (NB, NB), 1)
    ).astype(f32)

    def block(m, at):
        e_ref[m, :, :NB] = a_ref[m, at : at + NB, at : at + NB]
        e_ref[m, :, NB:] = eye

    def rest(m, o):
        n, c = o + NB, (o + NB) // 128 * 128
        t = dot3((w_ref[m, 0], w_ref[m, 1]), split(t_ref[m, o:n, :]))
        t_ref[m, o:n, :] = t
        if n < size:
            u = u_ref[m, 0, :, c:], u_ref[m, 1, :, c:]
            t_ref[m, n:, :] = t_ref[m, n:, :] - dot3(u, split(t), 0, 0)[n - c :]
            for r in range(c, size, 128):
                top = max(r, n)
                strip = u_ref[m, 0, :, r : r + 128], u_ref[m, 1, :, r : r + 128]
                right = u_ref[m, 0, :, r:], u_ref[m, 1, :, r:]
                change = dot3(strip, right, 0, 0)[top - r :]
                a_ref[m, top : r + 128, r:] = a_ref[m, top : r + 128, r:] - change

    for m in range(2):
        block(m, 0)
    for o in range(0, size, NB):
        n, c = o + NB, (o + NB) // 128 * 128
        chol_inverse(e_ref)
        if o > 0:
            for m in range(2):
                rest(m, o - NB)
        between(2)
        for m in range(2):
            w = split(e_ref[m, :, NB:])
            w_ref[m, 0], w_ref[m, 1] = w
            if n < size:
                u = split(dot3(w, split(a_ref[m, o:n, c:])))
                u_ref[m, 0, :, c:], u_ref[m, 1, :, c:] = u
                part = tuple(x[:, n - c : n - c + NB] for x in u)
                e_ref[m, :, :NB] = a_ref[m, n : n + NB, n : n + NB] - dot3(part, part, 0, 0)
                e_ref[m, :, NB:] = eye
        between()
    for m in range(2):
        rest(m, size - NB)


def main_kernel(
    nz, nf, order_ref, ids_ref, parts_hbm, mom_hbm, sec_hbm, lf_hbm, rf_hbm, lb_hbm, rb_hbm,
    held, grad_hbm,
    own_0, own_1, own_2, own_3, own_4, own_5, own_6, own_7, first_a, arms_a, first_b, arms_b, acc, out_a, grad_a, out_b, update,
    fac, bas, new, a_ref, t_ref, mom, sec, rotated, lq, rq, e_ref, back_hi,
    grad, lt, rt, w_ref, u_ref, keep_sem, load_sem, send_a, recv_a, send_b, recv_b, give_a, take_a, give_b, take_b, give_c, take_c,
):
    z = lax.axis_index("replica")
    f = lax.axis_index("fsdp")
    own = (own_0, own_1, own_2, own_3, own_4, own_5, own_6, own_7)
    group, rows, width = own_0.shape
    nref = ids_ref.shape[0]

    loads = [
        pltpu.make_async_copy(
            parts_hbm.at[0, pl.ds(lax.rem(z + k, nz) * group, group)], own[k], load_sem.at[k]
        )
        for k in range(nz)
    ]
    first_needed = (4, 3, 5)
    then_needed = (2, 6, 1, 7, 0)
    places = (
        (lf_hbm, fac.at[0]),
        (rf_hbm, fac.at[1]),
        (lb_hbm, bas.at[0]),
        (rb_hbm, bas.at[1]),
        (mom_hbm, mom),
        (sec_hbm, sec),
    )
    later = [
        pltpu.make_async_copy(src.at[0], dst, load_sem.at[nz + n])
        for n, (src, dst) in enumerate(places)
    ]
    for k in first_needed + then_needed:
        loads[k].start()

    barrier = pltpu.get_barrier_semaphore()
    for step in (1, nz - 1):
        pl.semaphore_signal(
            barrier, inc=1, device_id=(lax.rem(z + step, nz), f), device_id_type=MESH
        )

    def hello(i, c):
        pl.semaphore_signal(
            barrier, inc=1, device_id=(z, lax.rem(f + i, nf)), device_id_type=MESH
        )
        return c

    lax.fori_loop(1, nf, hello, 0)

    def early(g):
        start = (g * group) // DECADE
        found = []
        for c in range(EARLY):
            at = start + c
            block = jnp.where(at < nref, ids_ref[jnp.minimum(at, nref - 1)], nz * group)
            found.append(jnp.clip(block - g * group, 0, group - 1))
        return found

    def late(found, q):
        block = q
        for a in found:
            block = block + (block >= a).astype(jnp.int32)
        return block

    own_early = early(z)

    def position(block):
        block = jnp.clip(block, 0, group - 1)
        below = sum((a < block).astype(jnp.int32) for a in own_early)
        same = sum((a == block).astype(jnp.int32) for a in own_early)
        return jnp.where(same > 0, below, EARLY + block - below)

    for k in first_needed:
        loads[k].wait()
    pl.semaphore_wait(barrier, nf + 1)

    def target(way, arm, hop):
        left = HOPS[arm] - hop
        return nz - left if way == DOWN else left

    def ring_copy(stage, way, arm, hop, p):
        first, arms, send, recv, per = stage
        src = first.at[way, arm] if hop == 0 else arms.at[way, arm, hop - 1]
        step = nz - 1 if way == DOWN else 1
        piece = pl.ds(p * per, per)
        return pltpu.make_async_remote_copy(
            src_ref=src.at[piece],
            dst_ref=arms.at[way, arm, hop].at[piece],
            send_sem=send.at[way, arm, hop, p],
            recv_sem=recv.at[way, arm, hop, p],
            device_id=(lax.rem(z + step, nz), f),
            device_id_type=MESH,
        )

    def block_at(stage, k, part, i):
        found = early(lax.rem(z + k, nz))
        if stage is ring_a:
            return found[part * (EARLY // 2) + i]
        return late(found, part * ((group - EARLY) // 2) + i)

    def ring_step(stage, hop, p):
        first, arms, per = stage[0], stage[1], stage[4]
        for arm in (LONG, SHORT):
            if hop >= HOPS[arm]:
                continue
            for way in (DOWN, UP):
                if hop > 0:
                    ring_copy(stage, way, arm, hop - 1, p).wait_recv()
                dest = target(way, arm, hop)
                for k in range(per):
                    i = p * per + k
                    value = own[dest][block_at(stage, dest, way ^ arm, i)]
                    if hop == 0:
                        first[way, arm, i] = value
                    else:
                        total = arms[way, arm, hop - 1, i].astype(f32) + value.astype(f32)
                        arms[way, arm, hop - 1, i] = total.astype(bf16)
                ring_copy(stage, way, arm, hop, p).start()

    def ring_end(stage, p):
        arms, per = stage[1], stage[4]
        base = 0 if stage is ring_a else EARLY
        count = EARLY // 2 if stage is ring_a else (group - EARLY) // 2
        for part in range(2):
            long_way, short_way = (DOWN, UP) if part == 0 else (UP, DOWN)
            ring_copy(stage, long_way, LONG, 3, p).wait_recv()
            ring_copy(stage, short_way, SHORT, 2, p).wait_recv()
            for k in range(per):
                i = p * per + k
                total = (
                    arms[long_way, LONG, 3, i].astype(f32)
                    + arms[short_way, SHORT, 2, i].astype(f32)
                    + own[0][block_at(stage, 0, part, i)].astype(f32)
                )
                acc[base + part * count + i] = total.astype(bf16)

    def ring_sent(stage, pieces):
        for hop in range(4):
            for arm in (LONG, SHORT):
                if hop < HOPS[arm]:
                    for way in (DOWN, UP):

                        def sent(p, c):
                            ring_copy(stage, way, arm, hop, p).wait_send()
                            return c

                        lax.fori_loop(0, pieces, sent, 0)

    ring_a = (first_a, arms_a, send_a, recv_a, 1)
    ring_b = (first_b, arms_b, send_b, recv_b, PER)
    pieces = (group - EARLY) // 2 // PER
    todo = [functools.partial(ring_step, ring_b, hop, p) for hop in range(4) for p in range(pieces)]
    todo += [functools.partial(ring_end, ring_b, p) for p in range(pieces)]
    todo.append(lambda: to_owners(out_b, grad, give_b, take_b, group - 1))
    todo.reverse()

    def pump(n=1):
        for _ in range(n):
            if todo:
                todo.pop()()

    mine = pl.ds(pl.multiple_of(f * rows, rows), rows)

    def give(out, into, send, recv, i):
        return pltpu.make_async_remote_copy(
            src_ref=out.at[i],
            dst_ref=into.at[mine],
            send_sem=send.at[i],
            recv_sem=recv.at[i],
            device_id=(z, lax.rem(f + i, nf)),
            device_id_type=MESH,
        )

    def to_owners(out, into, send, recv, limit):
        def one(i, c):
            slot = lax.rem(f + i, nf)
            at = jnp.minimum(position(order_ref[z * group + slot] - z * group), limit)
            out[i] = acc[at]
            give(out, into, send, recv, i).start()
            return c

        lax.fori_loop(1, nf, one, 0)
        at = jnp.minimum(position(order_ref[z * group + f] - z * group), limit)
        into[mine] = acc[at]

    def from_all(out, into, send, recv):
        def one(i, c):
            give(out, into, send, recv, i).wait_recv()
            return c

        lax.fori_loop(1, nf, one, 0)

    for hop in range(4):
        for p in range(EARLY // 2):
            ring_step(ring_a, hop, p)
        pump(2 if hop else 1)
        if hop == 0:
            for k in then_needed:
                loads[k].wait()
            for load in later:
                load.start()
    for p in range(EARLY // 2):
        ring_end(ring_a, p)
    to_owners(out_a, grad_a, give_a, take_a, EARLY - 1)
    pump(5)
    for load in later:
        load.wait()
    from_all(out_a, grad_a, give_a, take_a)

    g_a = grad_a[...]
    for m in range(2):
        new[m] = 0.95 * fac[m] + (0.05 / width) * dg(g_a, g_a, 1 - m, 1 - m)
    pump()
    for m in range(2):
        t_ref[m] = dot3(split(bas[m]), split(new[m]), 0, 1)
    pump()
    for m in range(2):
        s = split(t_ref[m])
        a_ref[m] = dot3(s, s, 1, 1)
    pump()
    orthonormal(a_ref, t_ref, e_ref, w_ref, u_ref, pump)
    pump(len(todo))

    block = order_ref[z * group + f]
    flag = lax.fori_loop(
        0, nref, lambda i, c: c | (ids_ref[i] == block).astype(jnp.int32), jnp.int32(0)
    )
    refreshed = jnp.full((width, width), flag, jnp.int32) == 1
    for m, (q, t) in enumerate(((lq, lt), (rq, rt))):
        q[0], q[1] = split(jnp.where(refreshed, t_ref[m].T, bas[m]))
        t[0], t[1] = split(jnp.where(refreshed, t_ref[m], bas[m].T))
    half = split(dot3((lt[0], lt[1]), split(mom[...])))
    rotated[...] = 0.9 * dot3(half, (rq[0], rq[1]))
    from_all(out_b, grad, give_b, take_b)
    keep = pltpu.make_async_copy(grad, grad_hbm, keep_sem.at[0])
    keep.start()

    g = grad[...]
    turned = (dg(lt[0], g) + dg(lt[1], g)).astype(bf16)
    rot_grad = dg(turned, rq[0]) + dg(turned, rq[1])
    second = 0.95 * sec[...] + 0.05 * rot_grad * rot_grad
    scaled = ((rotated[...] + 0.1 * rot_grad) / (jnp.sqrt(second) + 1e-08)).astype(bf16)
    back_hi[...] = (dg(lq[0], scaled) + dg(lq[1], scaled)).astype(bf16)

    quarter = nf // 4

    def give_back(peer):
        there = pl.ds(pl.multiple_of(peer * rows, rows), rows)
        i = lax.rem(peer - f + nf, nf)
        return pltpu.make_async_remote_copy(
            src_ref=update.at[there],
            dst_ref=held.at[f],
            send_sem=give_c.at[i],
            recv_sem=take_c.at[i],
            device_id=(z, peer),
            device_id_type=MESH,
        )

    def some_rows(r, c):
        at = lax.rem(f // quarter + r, 4)
        span = pl.ds(pl.multiple_of(at * quarter * rows, quarter * rows), quarter * rows)
        chunk = back_hi[span]
        update[span] = (dg(chunk, rt[0]) + dg(chunk, rt[1])).astype(bf16)

        def one(i, c):
            peer = at * quarter + lax.rem(f + i, quarter)

            @pl.when(peer != f)
            def _():
                give_back(peer).start()

            return c

        lax.fori_loop(0, quarter, one, 0)
        return c

    lax.fori_loop(0, 4, some_rows, 0)
    stay = pltpu.make_async_copy(update.at[mine], held.at[f], keep_sem.at[1])
    stay.start()

    ring_sent(ring_a, EARLY // 2)
    ring_sent(ring_b, pieces)

    def drain(i, c):
        give(out_a, grad_a, give_a, take_a, i).wait_send()
        give(out_b, grad, give_b, take_b, i).wait_send()
        peer = lax.rem(f + i, nf)
        give_back(peer).wait_send()
        give_back(peer).wait_recv()
        return c

    lax.fori_loop(1, nf, drain, 0)
    stay.wait()
    keep.wait()


def main(nz, nf, order, ids, parts, *rest):
    _, blocks, rows, width = parts.shape
    group = blocks // nz
    smem = pl.BlockSpec(memory_space=pltpu.SMEM)
    hbm = pl.BlockSpec(memory_space=pl.ANY)
    square = pltpu.VMEM((width, width), f32)
    pair = pltpu.VMEM((2, width, width), f32)
    pair16 = pltpu.VMEM((2, width, width), bf16)
    square16 = pltpu.VMEM((width, width), bf16)
    slots = pltpu.VMEM((nf, rows, width), bf16)
    half_a, half_b = EARLY // 2, (group - EARLY) // 2
    ring = pltpu.SemaphoreType.DMA
    return pl.pallas_call(
        functools.partial(main_kernel, nz, nf),
        out_shape=(
            jax.ShapeDtypeStruct((nf, rows, width), bf16),
            jax.ShapeDtypeStruct((width, width), bf16),
        ),
        in_specs=[smem, smem] + [hbm] * 7,
        out_specs=(hbm, hbm),
        scratch_shapes=[
            *[pltpu.VMEM((group, rows, width), bf16)] * nz,
            pltpu.VMEM((2, 2, half_a, rows, width), bf16),
            pltpu.VMEM((2, 2, 4, half_a, rows, width), bf16),
            pltpu.VMEM((2, 2, half_b, rows, width), bf16),
            pltpu.VMEM((2, 2, 4, half_b, rows, width), bf16),
            slots,
            slots,
            square16,
            slots,
            square16,
            pair,
            pair,
            pair,
            pair,
            pair,
            square,
            square,
            square,
            pair16,
            pair16,
            pltpu.VMEM((2, NB, 2 * NB), f32),
            square16,
            square16,
            pair16,
            pair16,
            pltpu.VMEM((2, 2, NB, NB), bf16),
            pltpu.VMEM((2, 2, NB, width), bf16),
            ring((2,)),
            ring((nz + 6,)),
            ring((2, 2, 4, half_a)),
            ring((2, 2, 4, half_a)),
            ring((2, 2, 4, half_b // PER)),
            ring((2, 2, 4, half_b // PER)),
            ring((nf,)),
            ring((nf,)),
            ring((nf,)),
            ring((nf,)),
            ring((nf,)),
            ring((nf,)),
        ],
        compiler_params=pltpu.CompilerParams(
            collective_id=0, has_side_effects=True, vmem_limit_bytes=59 * 2**20
        ),
        name="soap_step",
    )(order, ids, parts, *rest)


def tail_kernel(nz, nf, order_ref, held, grad_hbm, lf_ref, rf_ref, out_hbm, ln_hbm, rn_hbm, grad_ref, rows, new, sem):
    z = lax.axis_index("replica")
    width = grad_ref.shape[1]
    group = held.shape[0]
    fetch = pltpu.make_async_copy(held, rows, sem.at[3 + nf])
    fetch.start()
    load = pltpu.make_async_copy(grad_hbm, grad_ref, sem.at[2 + nf])
    load.start()

    def place(i):
        block = jnp.clip(order_ref[z * group + i] - z * group, 0, group - 1)
        return pltpu.make_async_copy(rows.at[i], out_hbm.at[block], sem.at[2 + i])

    def begin(i, c):
        place(i).start()
        return c

    def end(i, c):
        place(i).wait()
        return c

    fetch.wait()
    lax.fori_loop(0, nf, begin, 0)
    load.wait()
    grad = grad_ref[...]
    stores = []
    for m, (fac, hbm) in enumerate(((lf_ref, ln_hbm), (rf_ref, rn_hbm))):
        new[m] = 0.95 * fac[0] + (0.05 / width) * dg(grad, grad, 1 - m, 1 - m)
        stores.append(pltpu.make_async_copy(new.at[m], hbm.at[0], sem.at[m]))
        stores[m].start()
    for store in stores:
        store.wait()
    lax.fori_loop(0, nf, end, 0)


def tail(nz, nf, order, held, grad, lf, rf):
    width = grad.shape[1]
    smem = pl.BlockSpec(memory_space=pltpu.SMEM)
    vmem = pl.BlockSpec(memory_space=pltpu.VMEM)
    hbm = pl.BlockSpec(memory_space=pl.ANY)
    whole = jax.ShapeDtypeStruct((1, width, width), f32)
    return pl.pallas_call(
        functools.partial(tail_kernel, nz, nf),
        out_shape=(jax.ShapeDtypeStruct(held.shape, bf16), whole, whole),
        in_specs=[smem, hbm, hbm, vmem, vmem],
        out_specs=(hbm, hbm, hbm),
        scratch_shapes=[
            pltpu.VMEM((width, width), bf16),
            pltpu.VMEM(held.shape, bf16),
            pltpu.VMEM((2, width, width), f32),
            pltpu.SemaphoreType.DMA((4 + nf,)),
        ],
        compiler_params=pltpu.CompilerParams(vmem_limit_bytes=63 * 2**20),
        name="write_out",
    )(order, held, grad, lf, rf)


def solution(mesh):
    nz, nf = mesh.shape["replica"], mesh.shape["fsdp"]

    def on_device(parts, moment, second, lf, rf, lb, rb, order, ids):
        held, grad = main(nz, nf, order, ids, parts, moment, second, lf, rf, lb, rb)
        return tail(nz, nf, order, held, grad, lf, rf)

    placed = (P("replica", None, "fsdp", None),) + (P(("replica", "fsdp"), None, None),) * 6 + (P(), P())
    return jax.shard_map(
        on_device,
        mesh=mesh,
        in_specs=placed,
        out_specs=(
            P("replica", "fsdp", None),
            P(("replica", "fsdp"), None, None),
            P(("replica", "fsdp"), None, None),
        ),
        check_vma=False,
    )
```

```python
import functools

import jax
import jax.numpy as jnp
from jax import lax
from jax.experimental import pallas as pl
from jax.experimental.pallas import tpu as pltpu
from jax.sharding import PartitionSpec as P

MESH = pl.DeviceIdType.MESH
f32 = jnp.float32
bf16 = jnp.bfloat16

DOWN, UP = 0, 1
LONG, SHORT = 0, 1
HOPS = (4, 3)
EARLY = 4
DECADE = 10
PER = 2
NB = 64


def split(x):
    high = x.astype(bf16)
    return high, (x - high.astype(f32)).astype(bf16)


def dg(a, b, ca=1, cb=0):
    return lax.dot_general(a, b, (((ca,), (cb,)), ((), ())), preferred_element_type=f32)


def dot3(a, b, ca=1, cb=0):
    return dg(a[0], b[0], ca, cb) + (dg(a[0], b[1], ca, cb) + dg(a[1], b[0], ca, cb))


def lanes(x, at):
    return [
        jnp.take_along_axis(x, jnp.full(x.shape, at + j, jnp.int32), axis=1) for j in range(8)
    ]


def spread(x, j):
    return jnp.broadcast_to(x[j : j + 1, :], x.shape)


def pivot_rows(e_ref, m, at):
    sub = lax.broadcasted_iota(jnp.int32, (8, 128), 0)
    piv = e_ref[m, at : at + 8, :]
    b = lanes(piv, at)
    diag = None
    inverse, above, pivots = [], [], []
    for j in range(8):
        d = spread(b[j], j)
        diag = d if diag is None else jnp.where(sub == j, d, diag)
        r = 1.0 / d
        inverse.append(r)
        factor = jnp.where(sub > j, b[j] * r, 0.0)
        row = {}
        for t in range(j + 1, 8):
            row[t] = spread(b[t], j)
            b[t] = b[t] - factor * row[t]
        above.append(row)
        pivots.append(spread(piv, j))
        piv = piv - factor * pivots[j]
    return inverse, above, pivots, piv * lax.rsqrt(diag)


def chol_inverse(e_ref):
    for at in range(0, NB, 8):
        found = [pivot_rows(e_ref, m, at) for m in range(2)]
        for m in range(2):
            inverse, above, pivots, piv = found[m]
            for i in range(at + 8, NB, 8):
                x = e_ref[m, i : i + 8, :]
                b = lanes(x, at)
                for j in range(8):
                    factor = b[j] * inverse[j]
                    for t in range(j + 1, 8):
                        b[t] = b[t] - factor * above[j][t]
                    x = x - factor * pivots[j]
                e_ref[m, i : i + 8, :] = x
            e_ref[m, at : at + 8, :] = piv


def orthonormal(a_ref, t_ref, e_ref, w_ref, u_ref, between):
    size = a_ref.shape[1]
    eye = (
        lax.broadcasted_iota(jnp.int32, (NB, NB), 0) == lax.broadcasted_iota(jnp.int32, (NB, NB), 1)
    ).astype(f32)

    def block(m, at):
        e_ref[m, :, :NB] = a_ref[m, at : at + NB, at : at + NB]
        e_ref[m, :, NB:] = eye

    def rest(m, o):
        n, c = o + NB, (o + NB) // 128 * 128
        t = dot3((w_ref[m, 0], w_ref[m, 1]), split(t_ref[m, o:n, :]))
        t_ref[m, o:n, :] = t
        if n < size:
            u = u_ref[m, 0, :, c:], u_ref[m, 1, :, c:]
            t_ref[m, n:, :] = t_ref[m, n:, :] - dot3(u, split(t), 0, 0)[n - c :]
            for r in range(c, size, 128):
                top = max(r, n)
                strip = u_ref[m, 0, :, r : r + 128], u_ref[m, 1, :, r : r + 128]
                right = u_ref[m, 0, :, r:], u_ref[m, 1, :, r:]
                change = dot3(strip, right, 0, 0)[top - r :]
                a_ref[m, top : r + 128, r:] = a_ref[m, top : r + 128, r:] - change

    for m in range(2):
        block(m, 0)
    for o in range(0, size, NB):
        n, c = o + NB, (o + NB) // 128 * 128
        chol_inverse(e_ref)
        if o > 0:
            for m in range(2):
                rest(m, o - NB)
        between(2)
        for m in range(2):
            w = split(e_ref[m, :, NB:])
            w_ref[m, 0], w_ref[m, 1] = w
            if n < size:
                u = split(dot3(w, split(a_ref[m, o:n, c:])))
                u_ref[m, 0, :, c:], u_ref[m, 1, :, c:] = u
                part = tuple(x[:, n - c : n - c + NB] for x in u)
                e_ref[m, :, :NB] = a_ref[m, n : n + NB, n : n + NB] - dot3(part, part, 0, 0)
                e_ref[m, :, NB:] = eye
        between()
    for m in range(2):
        rest(m, size - NB)


def main_kernel(
    nz, nf, order_ref, ids_ref, parts_hbm, mom_hbm, sec_hbm, lf_hbm, rf_hbm, lb_hbm, rb_hbm,
    held, grad_hbm,
    own_0, own_1, own_2, own_3, own_4, own_5, own_6, own_7, first_a, arms_a, first_b, arms_b, acc, out_a, grad_a, out_b, update,
    fac, bas, new, a_ref, t_ref, mom, sec, rotated, lq, rq, e_ref, back_hi,
    grad, lt, rt, w_ref, u_ref, keep_sem, load_sem, send_a, recv_a, send_b, recv_b, give_a, take_a, give_b, take_b, give_c, take_c,
):
    z = lax.axis_index("replica")
    f = lax.axis_index("fsdp")
    own = (own_0, own_1, own_2, own_3, own_4, own_5, own_6, own_7)
    group, rows, width = own_0.shape
    nref = ids_ref.shape[0]

    loads = [
        pltpu.make_async_copy(
            parts_hbm.at[0, pl.ds(lax.rem(z + k, nz) * group, group)], own[k], load_sem.at[k]
        )
        for k in range(nz)
    ]
    first_needed = (4, 3, 5)
    then_needed = (2, 6, 1, 7, 0)
    places = (
        (lf_hbm, fac.at[0]),
        (rf_hbm, fac.at[1]),
        (lb_hbm, bas.at[0]),
        (rb_hbm, bas.at[1]),
        (mom_hbm, mom),
        (sec_hbm, sec),
    )
    later = [
        pltpu.make_async_copy(src.at[0], dst, load_sem.at[nz + n])
        for n, (src, dst) in enumerate(places)
    ]
    for k in first_needed + then_needed:
        loads[k].start()

    barrier = pltpu.get_barrier_semaphore()
    for step in (1, nz - 1):
        pl.semaphore_signal(
            barrier, inc=1, device_id=(lax.rem(z + step, nz), f), device_id_type=MESH
        )

    def hello(i, c):
        pl.semaphore_signal(
            barrier, inc=1, device_id=(z, lax.rem(f + i, nf)), device_id_type=MESH
        )
        return c

    lax.fori_loop(1, nf, hello, 0)

    def early(g):
        start = (g * group) // DECADE
        found = []
        for c in range(EARLY):
            at = start + c
            block = jnp.where(at < nref, ids_ref[jnp.minimum(at, nref - 1)], nz * group)
            found.append(jnp.clip(block - g * group, 0, group - 1))
        return found

    def late(found, q):
        block = q
        for a in found:
            block = block + (block >= a).astype(jnp.int32)
        return block

    own_early = early(z)

    def position(block):
        block = jnp.clip(block, 0, group - 1)
        below = sum((a < block).astype(jnp.int32) for a in own_early)
        same = sum((a == block).astype(jnp.int32) for a in own_early)
        return jnp.where(same > 0, below, EARLY + block - below)

    for k in first_needed:
        loads[k].wait()
    pl.semaphore_wait(barrier, nf + 1)

    def target(way, arm, hop):
        left = HOPS[arm] - hop
        return nz - left if way == DOWN else left

    def ring_copy(stage, way, arm, hop, p):
        first, arms, send, recv, per = stage
        src = first.at[way, arm] if hop == 0 else arms.at[way, arm, hop - 1]
        step = nz - 1 if way == DOWN else 1
        piece = pl.ds(p * per, per)
        return pltpu.make_async_remote_copy(
            src_ref=src.at[piece],
            dst_ref=arms.at[way, arm, hop].at[piece],
            send_sem=send.at[way, arm, hop, p],
            recv_sem=recv.at[way, arm, hop, p],
            device_id=(lax.rem(z + step, nz), f),
            device_id_type=MESH,
        )

    def block_at(stage, k, part, i):
        found = early(lax.rem(z + k, nz))
        if stage is ring_a:
            return found[part * (EARLY // 2) + i]
        return late(found, part * ((group - EARLY) // 2) + i)

    def ring_step(stage, hop, p):
        first, arms, per = stage[0], stage[1], stage[4]
        for arm in (LONG, SHORT):
            if hop >= HOPS[arm]:
                continue
            for way in (DOWN, UP):
                if hop > 0:
                    ring_copy(stage, way, arm, hop - 1, p).wait_recv()
                dest = target(way, arm, hop)
                for k in range(per):
                    i = p * per + k
                    value = own[dest][block_at(stage, dest, way ^ arm, i)]
                    if hop == 0:
                        first[way, arm, i] = value
                    else:
                        total = arms[way, arm, hop - 1, i].astype(f32) + value.astype(f32)
                        arms[way, arm, hop - 1, i] = total.astype(bf16)
                ring_copy(stage, way, arm, hop, p).start()

    def ring_end(stage, p):
        arms, per = stage[1], stage[4]
        base = 0 if stage is ring_a else EARLY
        count = EARLY // 2 if stage is ring_a else (group - EARLY) // 2
        for part in range(2):
            long_way, short_way = (DOWN, UP) if part == 0 else (UP, DOWN)
            ring_copy(stage, long_way, LONG, 3, p).wait_recv()
            ring_copy(stage, short_way, SHORT, 2, p).wait_recv()
            for k in range(per):
                i = p * per + k
                total = (
                    arms[long_way, LONG, 3, i].astype(f32)
                    + arms[short_way, SHORT, 2, i].astype(f32)
                    + own[0][block_at(stage, 0, part, i)].astype(f32)
                )
                acc[base + part * count + i] = total.astype(bf16)

    def ring_sent(stage, pieces):
        for hop in range(4):
            for arm in (LONG, SHORT):
                if hop < HOPS[arm]:
                    for way in (DOWN, UP):

                        def sent(p, c):
                            ring_copy(stage, way, arm, hop, p).wait_send()
                            return c

                        lax.fori_loop(0, pieces, sent, 0)

    ring_a = (first_a, arms_a, send_a, recv_a, 1)
    ring_b = (first_b, arms_b, send_b, recv_b, PER)
    pieces = (group - EARLY) // 2 // PER
    todo = [functools.partial(ring_step, ring_b, hop, p) for hop in range(4) for p in range(pieces)]
    todo += [functools.partial(ring_end, ring_b, p) for p in range(pieces)]
    todo.append(lambda: to_owners(out_b, grad, give_b, take_b, group - 1))
    todo.reverse()

    def pump(n=1):
        for _ in range(n):
            if todo:
                todo.pop()()

    mine = pl.ds(pl.multiple_of(f * rows, rows), rows)

    def give(out, into, send, recv, i):
        return pltpu.make_async_remote_copy(
            src_ref=out.at[i],
            dst_ref=into.at[mine],
            send_sem=send.at[i],
            recv_sem=recv.at[i],
            device_id=(z, lax.rem(f + i, nf)),
            device_id_type=MESH,
        )

    def to_owners(out, into, send, recv, limit):
        def one(i, c):
            slot = lax.rem(f + i, nf)
            at = jnp.minimum(position(order_ref[z * group + slot] - z * group), limit)
            out[i] = acc[at]
            give(out, into, send, recv, i).start()
            return c

        lax.fori_loop(1, nf, one, 0)
        at = jnp.minimum(position(order_ref[z * group + f] - z * group), limit)
        into[mine] = acc[at]

    def from_all(out, into, send, recv):
        def one(i, c):
            give(out, into, send, recv, i).wait_recv()
            return c

        lax.fori_loop(1, nf, one, 0)

    for hop in range(4):
        for p in range(EARLY // 2):
            ring_step(ring_a, hop, p)
        pump(2 if hop else 1)
        if hop == 0:
            for k in then_needed:
                loads[k].wait()
            for load in later:
                load.start()
    for p in range(EARLY // 2):
        ring_end(ring_a, p)
    to_owners(out_a, grad_a, give_a, take_a, EARLY - 1)
    pump(5)
    for load in later:
        load.wait()
    from_all(out_a, grad_a, give_a, take_a)

    g_a = grad_a[...]
    for m in range(2):
        new[m] = 0.95 * fac[m] + (0.05 / width) * dg(g_a, g_a, 1 - m, 1 - m)
    pump()
    for m in range(2):
        t_ref[m] = dot3(split(bas[m]), split(new[m]), 0, 1)
    pump()
    for m in range(2):
        s = split(t_ref[m])
        a_ref[m] = dot3(s, s, 1, 1)
    pump()
    orthonormal(a_ref, t_ref, e_ref, w_ref, u_ref, pump)
    pump(len(todo))

    block = order_ref[z * group + f]
    flag = lax.fori_loop(
        0, nref, lambda i, c: c | (ids_ref[i] == block).astype(jnp.int32), jnp.int32(0)
    )
    refreshed = jnp.full((width, width), flag, jnp.int32) == 1
    for m, (q, t) in enumerate(((lq, lt), (rq, rt))):
        q[0], q[1] = split(jnp.where(refreshed, t_ref[m].T, bas[m]))
        t[0], t[1] = split(jnp.where(refreshed, t_ref[m], bas[m].T))
    half = split(dot3((lt[0], lt[1]), split(mom[...])))
    rotated[...] = 0.9 * dot3(half, (rq[0], rq[1]))
    from_all(out_b, grad, give_b, take_b)
    keep = pltpu.make_async_copy(grad, grad_hbm, keep_sem.at[0])
    keep.start()

    g = grad[...]
    turned = (dg(lt[0], g) + dg(lt[1], g)).astype(bf16)
    rot_grad = dg(turned, rq[0]) + dg(turned, rq[1])
    second = 0.95 * sec[...] + 0.05 * rot_grad * rot_grad
    scaled = ((rotated[...] + 0.1 * rot_grad) / (jnp.sqrt(second) + 1e-08)).astype(bf16)
    back_hi[...] = (dg(lq[0], scaled) + dg(lq[1], scaled)).astype(bf16)

    quarter = nf // 4

    def give_back(peer):
        there = pl.ds(pl.multiple_of(peer * rows, rows), rows)
        i = lax.rem(peer - f + nf, nf)
        return pltpu.make_async_remote_copy(
            src_ref=update.at[there],
            dst_ref=held.at[f],
            send_sem=give_c.at[i],
            recv_sem=take_c.at[i],
            device_id=(z, peer),
            device_id_type=MESH,
        )

    def some_rows(r, c):
        at = lax.rem(f // quarter + r, 4)
        span = pl.ds(pl.multiple_of(at * quarter * rows, quarter * rows), quarter * rows)
        chunk = back_hi[span]
        update[span] = (dg(chunk, rt[0]) + dg(chunk, rt[1])).astype(bf16)

        def one(i, c):
            peer = at * quarter + lax.rem(f + i, quarter)

            @pl.when(peer != f)
            def _():
                give_back(peer).start()

            return c

        lax.fori_loop(0, quarter, one, 0)
        return c

    lax.fori_loop(0, 4, some_rows, 0)
    stay = pltpu.make_async_copy(update.at[mine], held.at[f], keep_sem.at[1])
    stay.start()

    ring_sent(ring_a, EARLY // 2)
    ring_sent(ring_b, pieces)

    def drain(i, c):
        give(out_a, grad_a, give_a, take_a, i).wait_send()
        give(out_b, grad, give_b, take_b, i).wait_send()
        peer = lax.rem(f + i, nf)
        give_back(peer).wait_send()
        give_back(peer).wait_recv()
        return c

    lax.fori_loop(1, nf, drain, 0)
    stay.wait()
    keep.wait()


def main(nz, nf, order, ids, parts, *rest):
    _, blocks, rows, width = parts.shape
    group = blocks // nz
    smem = pl.BlockSpec(memory_space=pltpu.SMEM)
    hbm = pl.BlockSpec(memory_space=pl.ANY)
    square = pltpu.VMEM((width, width), f32)
    pair = pltpu.VMEM((2, width, width), f32)
    pair16 = pltpu.VMEM((2, width, width), bf16)
    square16 = pltpu.VMEM((width, width), bf16)
    slots = pltpu.VMEM((nf, rows, width), bf16)
    half_a, half_b = EARLY // 2, (group - EARLY) // 2
    ring = pltpu.SemaphoreType.DMA
    return pl.pallas_call(
        functools.partial(main_kernel, nz, nf),
        out_shape=(
            jax.ShapeDtypeStruct((nf, rows, width), bf16),
            jax.ShapeDtypeStruct((width, width), bf16),
        ),
        in_specs=[smem, smem] + [hbm] * 7,
        out_specs=(hbm, hbm),
        scratch_shapes=[
            *[pltpu.VMEM((group, rows, width), bf16)] * nz,
            pltpu.VMEM((2, 2, half_a, rows, width), bf16),
            pltpu.VMEM((2, 2, 4, half_a, rows, width), bf16),
            pltpu.VMEM((2, 2, half_b, rows, width), bf16),
            pltpu.VMEM((2, 2, 4, half_b, rows, width), bf16),
            slots,
            slots,
            square16,
            slots,
            square16,
            pair,
            pair,
            pair,
            pair,
            pair,
            square,
            square,
            square,
            pair16,
            pair16,
            pltpu.VMEM((2, NB, 2 * NB), f32),
            square16,
            square16,
            pair16,
            pair16,
            pltpu.VMEM((2, 2, NB, NB), bf16),
            pltpu.VMEM((2, 2, NB, width), bf16),
            ring((2,)),
            ring((nz + 6,)),
            ring((2, 2, 4, half_a)),
            ring((2, 2, 4, half_a)),
            ring((2, 2, 4, half_b // PER)),
            ring((2, 2, 4, half_b // PER)),
            ring((nf,)),
            ring((nf,)),
            ring((nf,)),
            ring((nf,)),
            ring((nf,)),
            ring((nf,)),
        ],
        compiler_params=pltpu.CompilerParams(
            collective_id=0, has_side_effects=True, vmem_limit_bytes=59 * 2**20
        ),
        name="soap_step",
    )(order, ids, parts, *rest)


def tail_kernel(nz, nf, order_ref, held, grad_hbm, lf_hbm, rf_hbm, out_hbm, ln_hbm, rn_hbm, grad_ref, rows, fac, new, sem):
    z = lax.axis_index("replica")
    width = grad_ref.shape[1]
    group = held.shape[0]
    fetch = pltpu.make_async_copy(held, rows, sem.at[3 + nf])
    fetch.start()
    load = pltpu.make_async_copy(grad_hbm, grad_ref, sem.at[2 + nf])
    load.start()
    olds = [
        pltpu.make_async_copy(hbm.at[0], fac.at[m], sem.at[4 + nf + m])
        for m, hbm in enumerate((lf_hbm, rf_hbm))
    ]
    for old in olds:
        old.start()

    def place(i):
        block = jnp.clip(order_ref[z * group + i] - z * group, 0, group - 1)
        return pltpu.make_async_copy(rows.at[i], out_hbm.at[block], sem.at[2 + i])

    def begin(i, c):
        place(i).start()
        return c

    def end(i, c):
        place(i).wait()
        return c

    fetch.wait()
    lax.fori_loop(0, nf, begin, 0)
    load.wait()
    grad = grad_ref[...]
    stores = []
    for m, hbm in enumerate((ln_hbm, rn_hbm)):
        olds[m].wait()
        new[m] = 0.95 * fac[m] + (0.05 / width) * dg(grad, grad, 1 - m, 1 - m)
        stores.append(pltpu.make_async_copy(new.at[m], hbm.at[0], sem.at[m]))
        stores[m].start()
    for store in stores:
        store.wait()
    lax.fori_loop(0, nf, end, 0)


def tail(nz, nf, order, held, grad, lf, rf):
    width = grad.shape[1]
    smem = pl.BlockSpec(memory_space=pltpu.SMEM)
    hbm = pl.BlockSpec(memory_space=pl.ANY)
    whole = jax.ShapeDtypeStruct((1, width, width), f32)
    return pl.pallas_call(
        functools.partial(tail_kernel, nz, nf),
        out_shape=(jax.ShapeDtypeStruct(held.shape, bf16), whole, whole),
        in_specs=[smem, hbm, hbm, hbm, hbm],
        out_specs=(hbm, hbm, hbm),
        scratch_shapes=[
            pltpu.VMEM((width, width), bf16),
            pltpu.VMEM(held.shape, bf16),
            pltpu.VMEM((2, width, width), f32),
            pltpu.VMEM((2, width, width), f32),
            pltpu.SemaphoreType.DMA((6 + nf,)),
        ],
        compiler_params=pltpu.CompilerParams(vmem_limit_bytes=63 * 2**20),
        name="write_out",
    )(order, held, grad, lf, rf)


def solution(mesh):
    nz, nf = mesh.shape["replica"], mesh.shape["fsdp"]

    def on_device(parts, moment, second, lf, rf, lb, rb, order, ids):
        held, grad = main(nz, nf, order, ids, parts, moment, second, lf, rf, lb, rb)
        return tail(nz, nf, order, held, grad, lf, rf)

    placed = (P("replica", None, "fsdp", None),) + (P(("replica", "fsdp"), None, None),) * 6 + (P(), P())
    return jax.shard_map(
        on_device,
        mesh=mesh,
        in_specs=placed,
        out_specs=(
            P("replica", "fsdp", None),
            P(("replica", "fsdp"), None, None),
            P(("replica", "fsdp"), None, None),
        ),
        check_vma=False,
    )
```
